256 devices in a mesh: row: 16 (over x_hi, z), col: 16 (over x_lo, y, core).
Axes of the slice: x: 4 (x_hi: 2, x_lo: 2; x = x_hi * 2 + x_lo), y: 4, z: 8, core: 2. Of those that a mesh axis runs over, the one named last changes fastest.
Arguments:
- charges: float32 [48, 64], P('row', 'col'), may hold values from -6 to 6
- hubbard: float32 [48, 64], P('row', 'col'), may hold values from 0.2 to 2
- coupling: float32 [3, 3], replicated, may hold values from 0.1 to 0.6
- orbital_atom: int32 [16, 16, 24], P('row', 'col'), may hold values from 0 to 11
- block_mask: int32 [64, 64], P('row', 'col'), may hold values from 0 to 1, as said below
- bare_ham: bfloat16 [6144, 6144], P('row', 'col'), as said below
- intersection: bfloat16 [6144, 6144], P('row', 'col'), as said below
Outputs:
- purified: float32 [6144, 6144], P('row', 'col')
The draws below stay inside these ranges and needn't reach their ends.
Inputs may be any that keep to these rules, and one draw needn't show every extreme that they name: `block_mask`: symmetric; blocks whose domain rows lie within 2 of each other, counted around the slab's periodic first dimension, are always occupied, other blocks only in part. `bare_ham`: symmetric. `intersection`: symmetric.
All inputs are finite; a program needn't handle non-finite values.
Results may differ from the reference program's by a relative error of at most 0.009.
Values may be sent and summed in bfloat16 or wider, within the bound.
No kernel may reach another device: no remote copies, remote signals or barrier semaphores. Data moves between devices by JAX's collectives and lax.ppermute only.
A program may use at most 64 MiB of HBM per device.

```python
import math
import jax
import jax.numpy as jnp

BLK = 96
ORBD = 24
ATOM_R = 3
ATOM_C = 4
ATOMS = 12
DOM_ROWS = 16
DOM_COLS = 16
GRID_R = 48
GRID_C = 64
ORB_ALL = 6144
NBLK = 64


def symmetric_normal(key, scale):
    values = jax.random.normal(key, (ORB_ALL, ORB_ALL), jnp.float32) * scale
    return (values + values.T) * 0.5 ** 0.5


def draw_bare_ham(key, part):
    key = jax.random.fold_in(key, 21)
    return symmetric_normal(key, ORB_ALL ** (-0.5)).astype(jnp.bfloat16)


def draw_intersection(key, part):
    key = jax.random.fold_in(key, 37)
    return symmetric_normal(key, ORB_ALL ** (-0.5)).astype(jnp.bfloat16)


def draw_block_mask(key, part):
    key = jax.random.fold_in(key, 53)
    blocks = jnp.arange(NBLK, dtype=jnp.int32)
    domain_row = blocks * BLK // ORBD // DOM_COLS
    apart = jnp.abs(domain_row[:, None] - domain_row[None, :])
    apart = jnp.minimum(apart, DOM_ROWS - apart)
    near = apart <= max(DOM_ROWS // 8, 1)
    picks = jax.random.randint(key, (NBLK, NBLK), 0, 8, dtype=jnp.int32)
    far = jnp.minimum(picks, picks.T) == 0
    return jnp.where(near | far, 1, 0).astype(jnp.int32)


def with_ends(values, stream_key, least, top_value):
    longest = values.shape.index(max(values.shape))
    spots = []
    for shift in (0, 1):
        where = [jax.random.randint(jax.random.fold_in(stream_key, axis), (), 0, length) for axis, length in enumerate(values.shape)]
        where[longest] = (where[longest] + shift) % values.shape[longest]
        spots.append(tuple(where))
    return values.at[spots[0]].set(least).at[spots[1]].set(top_value)


def level_of(own_key, dims, pieces, low, high):
    def one(dim, blocks):
        heights = jax.random.uniform(jax.random.fold_in(jax.random.fold_in(own_key, 6), dim), (blocks,), jnp.float32, low / len(pieces), high / len(pieces))
        return jnp.repeat(jnp.exp(heights), dims[dim] // blocks).reshape((-1,) + (1,) * (len(dims) - dim - 1))

    factor_of = one(*pieces[0])
    for cut in pieces[1:]:
        factor_of = factor_of * one(*cut)
    return factor_of


def scatter_about(key, shape, scale, most, cuts=(), kind=jnp.bfloat16):
    factor_of = level_of(key, shape, cuts, -0.22, 0.18) if cuts else 1.0
    entries = jax.random.normal(key, shape, jnp.float32) * scale * factor_of
    return jnp.minimum(jnp.maximum(entries, -most), most).astype(kind)


def setup_inputs(seed: int = 0) -> dict:
    keys = jax.random.split(jax.random.key(seed), 8)
    return {
        "charges": scatter_about(keys[0], (GRID_R, GRID_C), 1.0, 6.0, ((0, 16), (1, 16)), jnp.float32),
        "hubbard": jnp.clip(jnp.exp(math.log(2.0) - 2.3025851 * jax.random.uniform(keys[1], (GRID_R, GRID_C), jnp.float32) ** level_of(keys[1], (GRID_R, GRID_C), ((0, 16), (1, 16)), -0.2, 0.2)), 0.2, 2.0),
        "coupling": jnp.clip(jax.random.uniform(keys[2], (3, 3), jnp.float32, 0.1, 0.6), 0.1, 0.6),
        "orbital_atom": with_ends(jax.random.randint(keys[3], (DOM_ROWS, DOM_COLS, ORBD), 0, ATOMS), jax.random.fold_in(keys[3], 1), 0, ATOMS - 1).astype(jnp.int32),
        "block_mask": draw_block_mask(jax.random.fold_in(keys[7], 71), 0),
        "bare_ham": draw_bare_ham(jax.random.fold_in(keys[7], 71), 0),
        "intersection": draw_intersection(jax.random.fold_in(keys[7], 71), 0),
    }


def reference(charges, hubbard, coupling, orbital_atom, block_mask, bare_ham, intersection):
    shift_grid = hubbard * charges
    for a in range(3):
        for b in range(3):
            shift_grid = shift_grid + coupling[a, b] * jnp.roll(charges, (1 - a, 1 - b), axis=(0, 1))
    per_domain = shift_grid.reshape(DOM_ROWS, ATOM_R, DOM_COLS, ATOM_C).transpose(0, 2, 1, 3).reshape(DOM_ROWS, DOM_COLS, ATOMS)
    onehot = orbital_atom[:, :, :, None] == jnp.arange(ATOMS, dtype=jnp.int32)[None, None, None, :]
    orbital_shift = jnp.sum(jnp.where(onehot, per_domain[:, :, None, :], 0.0), axis=3).reshape(ORB_ALL)
    hamilton = bare_ham.astype(jnp.float32) + 0.5 * intersection.astype(jnp.float32) * (orbital_shift[:, None] + orbital_shift[None, :])
    full_mask = jnp.repeat(jnp.repeat(block_mask, BLK, axis=0), BLK, axis=1).astype(jnp.float32)
    identity = jnp.eye(ORB_ALL, dtype=jnp.float32)
    initial = (0.5 * identity - full_mask * hamilton).astype(jnp.bfloat16)
    square_term = jnp.dot(initial, initial, preferred_element_type=jnp.float32)
    square_half = square_term.astype(jnp.bfloat16)
    cube_term = jnp.dot(square_half, initial, preferred_element_type=jnp.float32)
    return 3.0 * square_term - 2.0 * cube_term
```

```python
import functools

import jax
import jax.numpy as jnp
from jax import lax
from jax.experimental import pallas as pl
from jax.experimental.pallas import tpu as pltpu
from jax.sharding import PartitionSpec as P

BLK = 96
TILE = 384
NROW = 16
ORBD = 24
LANES = 128
RING = 8
HIGH = lax.Precision.HIGHEST
F32 = jnp.float32
VMEM = pl.BlockSpec(memory_space=pltpu.VMEM)
SMEM = pl.BlockSpec(memory_space=pltpu.SMEM)
ANY = pl.BlockSpec(memory_space=pl.ANY)


def iota(shape, dim):
    return lax.broadcasted_iota(jnp.int32, shape, dim)


def pack_kernel(charges, hubbard, picks, out):
    col = lax.axis_index("col")
    out[...] = jnp.zeros_like(out)
    spread = (iota((4, LANES), 1) % 64 == 4 * col + iota((4, LANES), 0)).astype(F32)
    for first, ref in ((0, charges), (3, hubbard)):
        for i in range(3):
            row = jnp.zeros((1, LANES), F32)
            for j in range(4):
                row = row + spread[j : j + 1] * ref[i, j]
            out[first + i : first + i + 1, :] = row
    for part in range(3):
        lane = iota((1, LANES), 1) + part * LANES
        row = jnp.zeros((1, LANES), F32)
        for o in range(ORBD):
            row = jnp.where(lane == ORBD * col + o, picks[0, 0, o].astype(F32), row)
        out[6 + part : 7 + part, :] = row


def pack(charges, hubbard, orbital_atom):
    return pl.pallas_call(
        pack_kernel,
        out_shape=jax.ShapeDtypeStruct((16, LANES), F32),
        in_specs=[SMEM, SMEM, SMEM],
        out_specs=VMEM,
    )(charges, hubbard, orbital_atom)


def sum_kernel(parts, out):
    total = parts[0]
    for i in range(1, NROW):
        total = total + parts[i]
    out[...] = total


def sum_parts(parts):
    return pl.pallas_call(
        sum_kernel,
        out_shape=jax.ShapeDtypeStruct(parts.shape[1:], F32),
        in_specs=[VMEM],
        out_specs=VMEM,
    )(parts)


def everywhere(value, axis):
    copies = jnp.broadcast_to(value[None], (NROW,) + value.shape)
    return lax.all_to_all(copies, axis, 0, 0)


def row_shift(strips, coupling, q):
    above = strips[(q + NROW - 1) % NROW]
    here = strips[q]
    below = strips[(q + 1) % NROW]
    atoms = [above[2:3], here[0:1], here[1:2], here[2:3], below[0:1]]
    rolled = [[pltpu.roll(v, 1, 1), v, pltpu.roll(v, LANES - 1, 1)] for v in atoms]
    grids = []
    for i in range(3):
        shift = here[3 + i : 4 + i] * here[i : i + 1]
        for a in range(3):
            for b in range(3):
                shift = shift + coupling[a, b] * rolled[i + a][b]
        grids.append(shift)
    lane = iota((8, LANES), 0)
    grid = jnp.where(lane == 0, grids[0], jnp.where(lane == 1, grids[1], jnp.where(lane == 2, grids[2], 0.0)))
    picks = jnp.concatenate([here[6:7], here[7:8], here[8:9]], axis=1).astype(jnp.int32)
    orbital = iota((1, TILE), 1)
    atom_row = picks // 4
    atom_col = 4 * (orbital // ORBD) + picks % 4
    onehot = (iota((LANES, TILE), 0) == atom_col).astype(F32)
    by_row = jnp.dot(grid, onehot, precision=HIGH, preferred_element_type=F32)
    return jnp.sum(jnp.where(iota((8, TILE), 0) == atom_row, by_row, 0.0), axis=0, keepdims=True)


def initial_kernel(strips, coupling, mask, bare, inter, out):
    row = lax.axis_index("row")
    col = lax.axis_index("col")
    along_cols = row_shift(strips, coupling, col)
    along_rows = jnp.broadcast_to(row_shift(strips, coupling, row), (LANES, TILE)).T[:, :1]
    block = iota((1, TILE), 1) // BLK
    diagonal = jnp.where(row == col, 0.5, 0.0)
    for i in range(TILE // BLK):
        rows = slice(i * BLK, (i + 1) * BLK)
        keep = jnp.zeros((1, TILE), F32)
        for j in range(TILE // BLK):
            keep = jnp.where(block == j, mask[i, j].astype(F32), keep)
        ham = bare[rows, :].astype(F32) + 0.5 * inter[rows, :].astype(F32) * (along_rows[rows] + along_cols)
        eye = jnp.where(iota((BLK, TILE), 0) + i * BLK == iota((BLK, TILE), 1), diagonal, 0.0)
        out[rows, :] = (eye - keep * ham).astype(jnp.bfloat16)


def initial_tile(strips, coupling, mask, bare, inter):
    return pl.pallas_call(
        initial_kernel,
        out_shape=jax.ShapeDtypeStruct((TILE, TILE), jnp.bfloat16),
        in_specs=[VMEM, SMEM, SMEM, VMEM, VMEM],
        out_specs=VMEM,
        compiler_params=pltpu.CompilerParams(vmem_limit_bytes=32 << 20),
    )(strips, coupling, mask, bare, inter)


def ring_step(value, by):
    return lax.ppermute(value, "row", [(h * RING + i, h * RING + (i + by) % RING) for h in range(2) for i in range(RING)])


def column_tiles(tile):
    other = lax.ppermute(tile, "row", [(i, i ^ RING) for i in range(NROW)])
    found = [(0, 0, tile), (1, 0, other)]
    up, down = [tile, other], [tile, other]
    for step in (1, 2, 3):
        for half in (0, 1):
            up[half] = ring_step(up[half], 1)
            down[half] = ring_step(down[half], -1)
            found += [(half, step, up[half]), (half, -step, down[half])]
    found.append((0, 4, ring_step(up[0], 1)))
    found.append((1, -4, ring_step(down[1], -1)))
    return found


CHUNK = 4


def load(strip_ref, tile_refs, places, strip, column, sems):
    row = lax.axis_index("row")
    half, z = row // RING, row % RING
    copies = [pltpu.make_async_copy(strip_ref, strip, sems.at[0])]
    for n, (ref, (flip, distance)) in enumerate(zip(tile_refs, places)):
        k = (half + flip) % 2 * RING + (z - distance + RING) % RING
        to = column.at[pl.ds(pl.multiple_of(k * TILE, TILE), TILE), :]
        copies.append(pltpu.make_async_copy(ref, to, sems.at[n + 1]))
    for copy in copies:
        copy.start()
    for copy in copies:
        copy.wait()


def product(strip, column, acc):
    span = CHUNK * TILE
    for k in range(NROW // CHUNK):
        part = jnp.dot(strip[:, k * span : (k + 1) * span], column[k * span : (k + 1) * span, :], preferred_element_type=F32)
        if k == 0:
            acc[...] = part
        else:
            acc[...] += part


def square_kernel(places, strip_ref, *refs):
    tile_refs, (full, half, strip, column, sems) = refs[:NROW], refs[NROW:]
    load(strip_ref, tile_refs, places, strip, column, sems)
    product(strip, column, full)
    half[...] = full[...].astype(jnp.bfloat16)


def cube_kernel(places, strip_ref, square, *refs):
    tile_refs, (out, strip, column, acc, sems) = refs[:NROW], refs[NROW:]
    load(strip_ref, tile_refs, places, strip, column, sems)
    product(strip, column, acc)
    out[...] = 3.0 * square[...] - 2.0 * acc[...]


SCRATCH = [
    pltpu.VMEM((TILE, NROW * TILE), jnp.bfloat16),
    pltpu.VMEM((NROW * TILE, TILE), jnp.bfloat16),
]
SEMS = pltpu.SemaphoreType.DMA((NROW + 1,))
PARAMS = pltpu.CompilerParams(vmem_limit_bytes=40 << 20)
COST = pl.CostEstimate(flops=2 * TILE * TILE * TILE * NROW, bytes_accessed=4 * TILE * TILE * NROW, transcendentals=0)


def square_of(strip, tiles, places):
    return pl.pallas_call(
        functools.partial(square_kernel, places),
        out_shape=[jax.ShapeDtypeStruct((TILE, TILE), F32), jax.ShapeDtypeStruct((TILE, TILE), jnp.bfloat16)],
        in_specs=[ANY] * (1 + NROW),
        out_specs=[VMEM, VMEM],
        scratch_shapes=SCRATCH + [SEMS],
        compiler_params=PARAMS,
        cost_estimate=COST,
    )(strip, *tiles)


def purified_of(strip, square, tiles, places):
    return pl.pallas_call(
        functools.partial(cube_kernel, places),
        out_shape=jax.ShapeDtypeStruct((TILE, TILE), F32),
        in_specs=[ANY, VMEM] + [ANY] * NROW,
        out_specs=VMEM,
        scratch_shapes=SCRATCH + [pltpu.VMEM((TILE, TILE), F32), SEMS],
        compiler_params=PARAMS,
        cost_estimate=COST,
    )(strip, square, *tiles)


def per_device(charges, hubbard, coupling, orbital_atom, block_mask, bare_ham, intersection):
    packed = pack(charges, hubbard, orbital_atom)
    strip = sum_parts(everywhere(packed, "col"))
    strips = everywhere(strip, "row")
    initial = initial_tile(strips, coupling, block_mask, bare_ham, intersection)
    initial_strip = lax.all_gather(initial, "col", axis=1, tiled=True)
    found = column_tiles(initial)
    places = tuple((half, distance) for half, distance, _ in found)
    tiles = [tile for _, _, tile in found]
    square, square_half = square_of(initial_strip, tiles, places)
    square_strip = lax.all_gather(square_half, "col", axis=1, tiled=True)
    return purified_of(square_strip, square, tiles, places)


def solution(mesh):
    placed = (
        P("row", "col"),
        P("row", "col"),
        P(),
        P("row", "col", None),
        P("row", "col"),
        P("row", "col"),
        P("row", "col"),
    )
    return jax.shard_map(
        per_device, mesh=mesh, in_specs=placed, out_specs=P("row", "col"), check_vma=False
    )
```

```python
import functools

import jax
import jax.numpy as jnp
from jax import lax
from jax.experimental import pallas as pl
from jax.experimental.pallas import tpu as pltpu
from jax.sharding import PartitionSpec as P

BLK = 96
TILE = 384
NROW = 16
ORBD = 24
LANES = 128
RING = 8
HIGH = lax.Precision.HIGHEST
F32 = jnp.float32
VMEM = pl.BlockSpec(memory_space=pltpu.VMEM)
SMEM = pl.BlockSpec(memory_space=pltpu.SMEM)
ANY = pl.BlockSpec(memory_space=pl.ANY)


def iota(shape, dim):
    return lax.broadcasted_iota(jnp.int32, shape, dim)


def position(index):
    row, col = divmod(index, NROW)
    return row // RING, row % RING, col // RING, col % RING // 2, col % 2


def groups(key):
    found = {}
    for index in range(NROW * NROW):
        found.setdefault(key(*position(index)), []).append(index)
    return list(found.values())


PLANE = groups(lambda xh, z, xl, y, core: (z, core))
PILLAR = groups(lambda xh, z, xl, y, core: (xh, xl, y))


def pack_kernel(charges, hubbard, picks, mask, out):
    col = lax.axis_index("col")
    spread = (iota((4, LANES), 1) % 64 == 4 * col + iota((4, LANES), 0)).astype(F32)
    rows = []
    for ref, height in ((charges, 3), (hubbard, 3)):
        for i in range(height):
            row = jnp.zeros((1, LANES), F32)
            for j in range(4):
                row = row + spread[j : j + 1] * ref[i, j]
            rows.append(row)
    for part in range(3):
        lane = iota((1, LANES), 1) + part * LANES
        row = jnp.zeros((1, LANES), F32)
        for o in range(ORBD):
            row = jnp.where(lane == ORBD * col + o, picks[0, 0, o].astype(F32), row)
        rows.append(row)
    for i in range(4):
        row = jnp.zeros((1, LANES), F32)
        for j in range(4):
            row = row + spread[j : j + 1] * mask[i, j].astype(F32)
        rows.append(row)
    rows += [jnp.zeros((1, LANES), F32)] * (16 - len(rows))
    packed = jnp.concatenate(rows, axis=0)
    for n in range(NROW):
        out[n] = packed


def pack(charges, hubbard, orbital_atom, block_mask):
    return pl.pallas_call(
        pack_kernel,
        out_shape=jax.ShapeDtypeStruct((NROW, 16, LANES), F32),
        in_specs=[SMEM, SMEM, SMEM, SMEM],
        out_specs=VMEM,
    )(charges, hubbard, orbital_atom, block_mask)


def sum_kernel(parts, out):
    for half in range(2):
        total = parts[half * RING]
        for i in range(1, RING):
            total = total + parts[half * RING + i]
        for n in range(NROW):
            out[n, half] = total


def sum_parts(parts):
    return pl.pallas_call(
        sum_kernel,
        out_shape=jax.ShapeDtypeStruct((NROW, 2, 16, LANES), F32),
        in_specs=[VMEM],
        out_specs=VMEM,
    )(parts)


def exchange(copies, members):
    return lax.all_to_all(copies, ("row", "col"), 0, 0, axis_index_groups=members)


def domain_row(parts, q):
    half, z = q // RING, q % RING
    return parts[2 * z, half] + parts[2 * z + 1, half]


def row_shift(parts, coupling, q):
    above = domain_row(parts, (q + NROW - 1) % NROW)
    here = domain_row(parts, q)
    below = domain_row(parts, (q + 1) % NROW)
    atoms = [above[2:3], here[0:1], here[1:2], here[2:3], below[0:1]]
    rolled = [[pltpu.roll(v, 1, 1), v, pltpu.roll(v, LANES - 1, 1)] for v in atoms]
    grids = []
    for i in range(3):
        shift = here[3 + i : 4 + i] * here[i : i + 1]
        for a in range(3):
            for b in range(3):
                shift = shift + coupling[a, b] * rolled[i + a][b]
        grids.append(shift)
    line = iota((8, LANES), 0)
    grid = jnp.where(line == 0, grids[0], jnp.where(line == 1, grids[1], jnp.where(line == 2, grids[2], 0.0)))
    picks = jnp.concatenate([here[6:7], here[7:8], here[8:9]], axis=1).astype(jnp.int32)
    orbital = iota((1, TILE), 1)
    atom_row = picks // 4
    atom_col = 4 * (orbital // ORBD) + picks % 4
    onehot = (iota((LANES, TILE), 0) == atom_col).astype(F32)
    by_row = jnp.dot(grid, onehot, precision=HIGH, preferred_element_type=F32)
    return jnp.sum(jnp.where(iota((8, TILE), 0) == atom_row, by_row, 0.0), axis=0, keepdims=True)


def as_column(shift):
    return jnp.broadcast_to(shift, (LANES, TILE)).T


def kept(parts, row, col):
    blocks = domain_row(parts, row)[8:16]
    onehot = (iota((LANES, TILE), 0) == 4 * col + iota((LANES, TILE), 1) // BLK).astype(F32)
    return jnp.dot(blocks, onehot, preferred_element_type=F32)[1:5]


def form(out, bare, inter, keep, down, along, diagonal):
    for i in range(TILE // BLK):
        rows = slice(i * BLK, (i + 1) * BLK)
        ham = bare[rows, :].astype(F32) + 0.5 * inter[rows, :].astype(F32) * (down[rows, :1] + along)
        eye = jnp.where(iota((BLK, TILE), 0) + i * BLK == iota((BLK, TILE), 1), diagonal, 0.0)
        out[rows, :] = (eye - keep[i : i + 1] * ham).astype(jnp.bfloat16)


def initial_kernel(parts, coupling, raw, other, out, out_other):
    row, col = lax.axis_index("row"), lax.axis_index("col")
    along = row_shift(parts, coupling, col)
    for q, source, to in ((row, raw, out), ((row + RING) % NROW, other, out_other)):
        down = as_column(row_shift(parts, coupling, q))
        form(to, source.at[:, :TILE], source.at[:, TILE:], kept(parts, q, col), down, along, jnp.where(q == col, 0.5, 0.0))


BIG = pltpu.CompilerParams(vmem_limit_bytes=56 << 20)


def initial_tiles(parts, coupling, raw, other):
    return pl.pallas_call(
        initial_kernel,
        out_shape=[jax.ShapeDtypeStruct((TILE, TILE), jnp.bfloat16)] * 2,
        in_specs=[VMEM, SMEM, VMEM, VMEM],
        out_specs=[VMEM, VMEM],
        compiler_params=BIG,
    )(parts, coupling, raw, other)


def strip_kernel(parts, coupling, after, raw, out, down):
    row, col = lax.axis_index("row"), pl.program_id(0)

    @pl.when(col == 0)
    def _():
        down[...] = as_column(row_shift(parts, coupling, row))

    along = row_shift(parts, coupling, col)
    form(out, raw.at[:, :TILE], raw.at[:, TILE:], kept(parts, row, col), down, along, jnp.where(row == col, 0.5, 0.0))


def initial_strip_of(parts, coupling, raw_strip, after):
    return pl.pallas_call(
        strip_kernel,
        grid=(NROW,),
        out_shape=jax.ShapeDtypeStruct((TILE, NROW * TILE), jnp.bfloat16),
        in_specs=[VMEM, SMEM, ANY, pl.BlockSpec((TILE, 2 * TILE), lambda k: (0, k))],
        out_specs=pl.BlockSpec((TILE, TILE), lambda k: (0, k)),
        scratch_shapes=[pltpu.VMEM((TILE, LANES), F32)],
        compiler_params=BIG,
        cost_estimate=pl.CostEstimate(flops=20 * TILE * TILE * NROW, bytes_accessed=6 * TILE * TILE * NROW, transcendentals=0),
    )(parts, coupling, after, raw_strip)


def ring_step(value, by):
    return lax.ppermute(value, "row", [(h * RING + i, h * RING + (i + by) % RING) for h in range(2) for i in range(RING)])


def swap_half(value):
    return lax.ppermute(value, "row", [(i, i ^ RING) for i in range(NROW)])


def column_tiles(tile, other):
    found = [(0, 0, tile), (1, 0, other)]
    up, down = [tile, other], [tile, other]
    for step in (1, 2, 3):
        for half in (0, 1):
            up[half] = ring_step(up[half], 1)
            down[half] = ring_step(down[half], -1)
            found += [(half, step, up[half]), (half, -step, down[half])]
    found.append((0, 4, ring_step(up[0], 1)))
    found.append((1, -4, ring_step(down[1], -1)))
    return found, up[1]


CHUNK = 4


def load(strip_ref, tile_refs, places, strip, column, sems):
    row = lax.axis_index("row")
    half, z = row // RING, row % RING
    copies = [pltpu.make_async_copy(strip_ref, strip, sems.at[0])]
    for n, (ref, (flip, distance)) in enumerate(zip(tile_refs, places)):
        k = (half + flip) % 2 * RING + (z - distance + RING) % RING
        to = column.at[pl.ds(pl.multiple_of(k * TILE, TILE), TILE), :]
        copies.append(pltpu.make_async_copy(ref, to, sems.at[n + 1]))
    for copy in copies:
        copy.start()
    for copy in copies:
        copy.wait()


def product(strip, column, acc):
    span = CHUNK * TILE
    for k in range(NROW // CHUNK):
        part = jnp.dot(strip[:, k * span : (k + 1) * span], column[k * span : (k + 1) * span, :], preferred_element_type=F32)
        if k == 0:
            acc[...] = part
        else:
            acc[...] += part


def square_kernel(places, strip_ref, *refs):
    tile_refs, (full, half, strip, column, sems) = refs[:NROW], refs[NROW:]
    load(strip_ref, tile_refs, places, strip, column, sems)
    product(strip, column, full)
    half[...] = full[...].astype(jnp.bfloat16)


def cube_kernel(places, strip_ref, square, *refs):
    tile_refs, (out, strip, column, acc, sems) = refs[:NROW], refs[NROW:]
    load(strip_ref, tile_refs, places, strip, column, sems)
    product(strip, column, acc)
    out[...] = 3.0 * square[...] - 2.0 * acc[...]


SCRATCH = [
    pltpu.VMEM((TILE, NROW * TILE), jnp.bfloat16),
    pltpu.VMEM((NROW * TILE, TILE), jnp.bfloat16),
]
SEMS = pltpu.SemaphoreType.DMA((NROW + 1,))
COST = pl.CostEstimate(flops=2 * TILE * TILE * TILE * NROW, bytes_accessed=4 * TILE * TILE * NROW, transcendentals=0)


def square_of(strip, tiles, places):
    return pl.pallas_call(
        functools.partial(square_kernel, places),
        out_shape=[jax.ShapeDtypeStruct((TILE, TILE), F32), jax.ShapeDtypeStruct((TILE, TILE), jnp.bfloat16)],
        in_specs=[ANY] * (1 + NROW),
        out_specs=[VMEM, VMEM],
        scratch_shapes=SCRATCH + [SEMS],
        compiler_params=BIG,
        cost_estimate=COST,
    )(strip, *tiles)


def purified_of(strip, square, tiles, places):
    return pl.pallas_call(
        functools.partial(cube_kernel, places),
        out_shape=jax.ShapeDtypeStruct((TILE, TILE), F32),
        in_specs=[ANY, VMEM] + [ANY] * NROW,
        out_specs=VMEM,
        scratch_shapes=SCRATCH + [pltpu.VMEM((TILE, TILE), F32), SEMS],
        compiler_params=BIG,
        cost_estimate=COST,
    )(strip, square, *tiles)


def per_device(charges, hubbard, coupling, orbital_atom, block_mask, bare_ham, intersection):
    raw = jnp.concatenate([bare_ham, intersection], axis=1)
    raw_strip = lax.all_gather(raw, "col", axis=1, tiled=True)
    raw_other = swap_half(raw)
    parts = exchange(pack(charges, hubbard, orbital_atom, block_mask), PLANE)
    parts = exchange(sum_parts(parts), PILLAR)
    initial, initial_other = initial_tiles(parts, coupling, raw, raw_other)
    found, late = column_tiles(initial, initial_other)
    initial_strip = initial_strip_of(parts, coupling, raw_strip, late)
    places = tuple((half, distance) for half, distance, _ in found)
    tiles = [tile for _, _, tile in found]
    square, square_half = square_of(initial_strip, tiles, places)
    square_strip = lax.all_gather(square_half, "col", axis=1, tiled=True)
    return purified_of(square_strip, square, tiles, places)


def solution(mesh):
    placed = (
        P("row", "col"),
        P("row", "col"),
        P(),
        P("row", "col", None),
        P("row", "col"),
        P("row", "col"),
        P("row", "col"),
    )
    return jax.shard_map(
        per_device, mesh=mesh, in_specs=placed, out_specs=P("row", "col"), check_vma=False
    )
```

```python
import functools

import jax
import jax.numpy as jnp
from jax import lax
from jax.experimental import pallas as pl
from jax.experimental.pallas import tpu as pltpu
from jax.sharding import PartitionSpec as P

BLK = 96
TILE = 384
NROW = 16
ORBD = 24
LANES = 128
RING = 8
HIGH = lax.Precision.HIGHEST
F32 = jnp.float32
VMEM = pl.BlockSpec(memory_space=pltpu.VMEM)
SMEM = pl.BlockSpec(memory_space=pltpu.SMEM)
ANY = pl.BlockSpec(memory_space=pl.ANY)


def iota(shape, dim):
    return lax.broadcasted_iota(jnp.int32, shape, dim)


def position(index):
    row, col = divmod(index, NROW)
    return row // RING, row % RING, col // RING, col % RING // 2, col % 2


def groups(key):
    found = {}
    for index in range(NROW * NROW):
        found.setdefault(key(*position(index)), []).append(index)
    return list(found.values())


PLANE = groups(lambda xh, z, xl, y, core: (z, core))
PILLAR = groups(lambda xh, z, xl, y, core: (xh, xl, y))


def pack_kernel(charges, hubbard, picks, mask, out):
    values = [charges[i, j] for i in range(3) for j in range(4)]
    values += [hubbard[i, j] for i in range(3) for j in range(4)]
    values += [picks[0, 0, o].astype(F32) for o in range(ORBD)]
    values += [mask[i, j].astype(F32) for i in range(4) for j in range(4)]
    lane = iota((1, LANES), 1)
    row = jnp.zeros((1, LANES), F32)
    for n, value in enumerate(values):
        row = jnp.where(lane == n, value, row)
    for n in range(NROW):
        out[n] = row


def pack(charges, hubbard, orbital_atom, block_mask):
    return pl.pallas_call(
        pack_kernel,
        out_shape=jax.ShapeDtypeStruct((NROW, 1, LANES), F32),
        in_specs=[SMEM, SMEM, SMEM, SMEM],
        out_specs=VMEM,
    )(charges, hubbard, orbital_atom, block_mask)


def copy_kernel(parts, bare_other, inter_other, out):
    rows = jnp.concatenate([parts[n] for n in range(NROW)], axis=0)
    for n in range(NROW):
        out[n] = rows


def copies_of(parts, bare_other, inter_other):
    return pl.pallas_call(
        copy_kernel,
        out_shape=jax.ShapeDtypeStruct((NROW, NROW, LANES), F32),
        in_specs=[VMEM, ANY, ANY],
        out_specs=VMEM,
    )(parts, bare_other, inter_other)


def exchange(copies, members):
    return lax.all_to_all(copies, ("row", "col"), 0, 0, axis_index_groups=members)


def spread_of():
    value = iota((LANES, LANES), 0)
    lane = iota((LANES, LANES), 1)
    parts = [value == 4 * i + lane % 4 for i in range(6)]
    parts += [value == 24 + (lane + LANES * i) % ORBD for i in range(3)]
    parts += [value == 48 + 4 * i + lane % 4 for i in range(4)]
    return jnp.concatenate([part.astype(F32) for part in parts], axis=1)


def domain_row(parts, spread, q):
    half, z = q // RING, q % RING
    domain = iota((NROW, LANES), 0)
    lane = iota((NROW, LANES), 1)
    block = parts[pl.ds(half * RING, RING), pl.ds(z * 2, 2), :]
    block = jnp.concatenate([block[n // 2, n % 2 : n % 2 + 1] for n in range(NROW)], axis=0)
    wide = jnp.dot(block, spread, precision=HIGH, preferred_element_type=F32)
    rows = []
    for i in range(13):
        here = lane % 64 // 4 == domain
        if 6 <= i < 9:
            here = (lane + LANES * (i - 6)) // ORBD == domain
        piece = wide[:, i * LANES : (i + 1) * LANES]
        rows.append(jnp.sum(jnp.where(here, piece, 0.0), axis=0, keepdims=True))
    return rows


def row_shift(above, here, below, coupling):
    atoms = [above[2], here[0], here[1], here[2], below[0]]
    rolled = [[pltpu.roll(v, 1, 1), v, pltpu.roll(v, LANES - 1, 1)] for v in atoms]
    grids = []
    for i in range(3):
        shift = here[3 + i] * here[i]
        for a in range(3):
            for b in range(3):
                shift = shift + coupling[a, b] * rolled[i + a][b]
        grids.append(shift)
    line = iota((8, LANES), 0)
    grid = jnp.where(line == 0, grids[0], jnp.where(line == 1, grids[1], jnp.where(line == 2, grids[2], 0.0)))
    picks = jnp.concatenate(here[6:9], axis=1).astype(jnp.int32)
    orbital = iota((1, TILE), 1)
    atom_row = picks // 4
    atom_col = 4 * (orbital // ORBD) + picks % 4
    onehot = (iota((LANES, TILE), 0) == atom_col).astype(F32)
    by_row = jnp.dot(grid, onehot, precision=HIGH, preferred_element_type=F32)
    return jnp.sum(jnp.where(iota((8, TILE), 0) == atom_row, by_row, 0.0), axis=0, keepdims=True)


def as_column(shift):
    return jnp.broadcast_to(shift, (LANES, TILE)).T


def kept(here, col):
    blocks = jnp.concatenate(here[9:13] * 2, axis=0)
    onehot = (iota((LANES, TILE), 0) == 4 * col + iota((LANES, TILE), 1) // BLK).astype(F32)
    return jnp.dot(blocks, onehot, preferred_element_type=F32)


def form(out, bare, inter, keep, down, along, diagonal):
    for i in range(TILE // BLK):
        rows = slice(i * BLK, (i + 1) * BLK)
        ham = bare[rows, :].astype(F32) + 0.5 * inter[rows, :].astype(F32) * (down[rows, :1] + along)
        eye = jnp.where(iota((BLK, TILE), 0) + i * BLK == iota((BLK, TILE), 1), diagonal, 0.0)
        out[rows, :] = (eye - keep[i : i + 1] * ham).astype(jnp.bfloat16)


def initial_kernel(parts, coupling, bare, inter, bare_other, inter_other, out, out_other):
    row, col = lax.axis_index("row"), lax.axis_index("col")
    spread = spread_of()

    def around(q):
        return [domain_row(parts, spread, (q + by) % NROW) for by in (NROW - 1, 0, 1)]

    along = row_shift(*around(col), coupling)
    for q, ham, overlap, to in ((row, bare, inter, out), ((row + RING) % NROW, bare_other, inter_other, out_other)):
        near = around(q)
        down = as_column(row_shift(*near, coupling))
        form(to, ham, overlap, kept(near[1], col), down, along, jnp.where(q == col, 0.5, 0.0))


BIG = pltpu.CompilerParams(vmem_limit_bytes=62 << 20)


def initial_tiles(parts, coupling, *sources):
    return pl.pallas_call(
        initial_kernel,
        out_shape=[jax.ShapeDtypeStruct((TILE, TILE), jnp.bfloat16)] * 2,
        in_specs=[VMEM, SMEM] + [VMEM] * 4,
        out_specs=[VMEM, VMEM],
        compiler_params=BIG,
    )(parts, coupling, *sources)


def ring_step(value, by):
    return lax.ppermute(value, "row", [(h * RING + i, h * RING + (i + by) % RING) for h in range(2) for i in range(RING)])


def swap_half(value):
    return lax.ppermute(value, "row", [(i, i ^ RING) for i in range(NROW)])


def column_tiles(tile, other):
    found = {(0, 0): tile, (1, 0): other}
    up, down = [tile, other], [tile, other]
    for step in (1, 2, 3):
        for half in (0, 1):
            up[half] = ring_step(up[half], 1)
            down[half] = ring_step(down[half], -1)
            found[half, step] = up[half]
            found[half, RING - step] = down[half]
    found[0, 4] = ring_step(up[0], 1)
    found[1, 4] = ring_step(down[1], -1)
    return found


def plane_step(value, flip, by):
    pairs = []
    for index in range(NROW):
        half, y, core = index // RING, index % RING // 2, index % 2
        pairs.append((index, (half ^ flip) * RING + (y + by) % 4 * 2 + core))
    return lax.ppermute(value, "col", pairs)


def swap_core(value):
    return lax.ppermute(value, "col", [(i, i ^ 1) for i in range(NROW)])


def square_tiles(tile):
    other = plane_step(tile, 1, 0)
    found = [(0, 0, tile), (1, 0, other)]
    for by in (1, 3, 2):
        found.append((0, by, plane_step(tile, 0, by)))
    far = found[-1][2]
    for by in (1, 3):
        found.append((1, by, plane_step(other, 0, by)))
    found.append((1, 2, plane_step(far, 1, 0)))
    return [(flip, by, side, swap_core(value) if side else value) for flip, by, value in found for side in (0, 1)]


def run(copies):
    for copy in copies:
        copy.start()
    return copies


def settle(copies):
    for copy in copies:
        copy.wait()


def square_kernel(places, first, *refs):
    count = len(places)
    strip_ref, *refs = refs
    held = [] if first else [refs.pop(0)]
    tile_refs, refs = refs[:count], refs[count:]
    outs, (strip, column, sems) = refs[:-3], refs[-3:]
    row = lax.axis_index("row")
    own, z = row // RING, row % RING
    copies = []
    for n, (half, distance) in enumerate(places):
        k = (own + half) % 2 * RING + (z - distance + RING) % RING
        source = strip_ref.at[:, pl.ds(pl.multiple_of(k * TILE, TILE), TILE)]
        copies.append(pltpu.make_async_copy(tile_refs[n], column.at[n * TILE : (n + 1) * TILE, :], sems.at[2 * n]))
        copies.append(pltpu.make_async_copy(source, strip.at[:, n * TILE : (n + 1) * TILE], sems.at[2 * n + 1]))
    run(copies)
    for n in range(0, count, 4):
        upto = min(n + 4, count)
        settle(copies[2 * n : 2 * upto])
        span = slice(n * TILE, upto * TILE)
        part = jnp.dot(strip[:, span], column[span, :], preferred_element_type=F32)
        if n == 0 and not held:
            outs[0][...] = part
        else:
            outs[0][...] = (held[0][...] if n == 0 else outs[0][...]) + part
    if not first:
        outs[1][...] = outs[0][...].astype(jnp.bfloat16)


def square_of(strip, held, found, places):
    count = len(places)
    shapes = [jax.ShapeDtypeStruct((TILE, TILE), F32)]
    if held:
        shapes.append(jax.ShapeDtypeStruct((TILE, TILE), jnp.bfloat16))
    return pl.pallas_call(
        functools.partial(square_kernel, places, not held),
        out_shape=shapes,
        in_specs=[ANY] + [VMEM] * len(held) + [ANY] * count,
        out_specs=[VMEM] * len(shapes),
        scratch_shapes=[
            pltpu.VMEM((TILE, count * TILE), jnp.bfloat16),
            pltpu.VMEM((count * TILE, TILE), jnp.bfloat16),
            pltpu.SemaphoreType.DMA((2 * count,)),
        ],
        compiler_params=BIG,
        cost_estimate=cost(count),
    )(strip, *held, *[found[place] for place in places])


def cost(count):
    return pl.CostEstimate(flops=2 * count * TILE**3, bytes_accessed=4 * count * TILE**2, transcendentals=0)


ORDER = tuple((half, 2 * step + odd) for odd in (0, 1) for half in (0, 1) for step in range(4))
LAST = ((0, 4), (1, 4))
FIRST = tuple(place for place in ORDER if place not in LAST)


def rows_for(flip, by, side):
    row, col = lax.axis_index("row"), lax.axis_index("col")
    k = (col // RING + flip) % 2 * RING + (col % RING // 2 - by + 4) % 4 * 2 + (col + side) % 2
    half, distance = (k // RING + row // RING) % 2, (row % RING - k % RING + RING) % RING
    return pl.ds(pl.multiple_of((distance % 2 * 8 + half * 4 + distance // 2) * TILE, TILE), TILE)


def early_kernel(early, late, *refs):
    count = len(early)
    tile_refs, column_refs, refs = refs[:count], refs[count : count + NROW], refs[count + NROW :]
    out, rest, strip, column, sems, rest_sems = refs
    copies = [pltpu.make_async_copy(ref, column.at[n * TILE : (n + 1) * TILE, :], sems.at[n]) for n, ref in enumerate(column_refs)]
    for n, ref in enumerate(tile_refs):
        copies.append(pltpu.make_async_copy(ref, strip.at[:, n * TILE : (n + 1) * TILE], sems.at[NROW + n]))
    settle(run(copies))
    leaving = []
    for n, place in enumerate(late):
        to = rest.at[n * TILE : (n + 1) * TILE, :]
        leaving.append(pltpu.make_async_copy(column.at[rows_for(*place), :], to, rest_sems.at[n]))
    run(leaving)
    for n, place in enumerate(early):
        part = jnp.dot(strip[:, n * TILE : (n + 1) * TILE], column[rows_for(*place), :], preferred_element_type=F32)
        if n == 0:
            out[...] = part
        else:
            out[...] += part
    settle(leaving)


def early_of(tiles, columns, early, late):
    count = len(early)
    return pl.pallas_call(
        functools.partial(early_kernel, early, late),
        out_shape=[
            jax.ShapeDtypeStruct((TILE, TILE), F32),
            jax.ShapeDtypeStruct((len(late) * TILE, TILE), jnp.bfloat16),
        ],
        in_specs=[ANY] * (count + NROW),
        out_specs=[VMEM, ANY],
        scratch_shapes=[
            pltpu.VMEM((TILE, count * TILE), jnp.bfloat16),
            pltpu.VMEM((NROW * TILE, TILE), jnp.bfloat16),
            pltpu.SemaphoreType.DMA((NROW + count,)),
            pltpu.SemaphoreType.DMA((len(late),)),
        ],
        compiler_params=BIG,
        cost_estimate=cost(NROW),
    )(*tiles, *columns)


def late_kernel(count, square_ref, held_ref, rest_ref, *refs):
    tile_refs, (out, square, held, rest, strip, sems) = refs[:count], refs[count:]
    copies = [pltpu.make_async_copy(ref, strip.at[:, n * TILE : (n + 1) * TILE], sems.at[n]) for n, ref in enumerate(tile_refs)]
    for n, (ref, to) in enumerate(((rest_ref, rest), (square_ref, square), (held_ref, held))):
        copies.append(pltpu.make_async_copy(ref, to, sems.at[count + n]))
    settle(run(copies))
    part = jnp.dot(strip[...], rest[...], preferred_element_type=F32)
    out[...] = 3.0 * square[...] - 2.0 * (held[...] + part)


def late_of(square, held, rest, tiles):
    count = len(tiles)
    return pl.pallas_call(
        functools.partial(late_kernel, count),
        out_shape=jax.ShapeDtypeStruct((TILE, TILE), F32),
        in_specs=[ANY] * (3 + count),
        out_specs=VMEM,
        scratch_shapes=[
            pltpu.VMEM((TILE, TILE), F32),
            pltpu.VMEM((TILE, TILE), F32),
            pltpu.VMEM((count * TILE, TILE), jnp.bfloat16),
            pltpu.VMEM((TILE, count * TILE), jnp.bfloat16),
            pltpu.SemaphoreType.DMA((3 + count,)),
        ],
        compiler_params=BIG,
        cost_estimate=cost(count),
    )(square, held, rest, *tiles)


EARLY = 10


def per_device(charges, hubbard, coupling, orbital_atom, block_mask, bare_ham, intersection):
    bare_other, intersection_other = swap_half(bare_ham), swap_half(intersection)
    parts = exchange(pack(charges, hubbard, orbital_atom, block_mask), PILLAR)
    parts = exchange(copies_of(parts, bare_other, intersection_other), PLANE)
    initial, initial_other = initial_tiles(parts, coupling, bare_ham, intersection, bare_other, intersection_other)
    initial_strip = lax.all_gather(initial, "col", axis=1, tiled=True)
    found = column_tiles(initial, initial_other)
    held = square_of(initial_strip, [], found, FIRST)
    square, square_low = square_of(initial_strip, held, found, LAST)
    tiles = square_tiles(square_low)
    places, values = [tile[:3] for tile in tiles], [tile[3] for tile in tiles]
    held, rest = early_of(values[:EARLY], [found[place] for place in ORDER], places[:EARLY], places[EARLY:])
    return late_of(square, held, rest, values[EARLY:])


def solution(mesh):
    placed = (
        P("row", "col"),
        P("row", "col"),
        P(),
        P("row", "col", None),
        P("row", "col"),
        P("row", "col"),
        P("row", "col"),
    )
    return jax.shard_map(
        per_device, mesh=mesh, in_specs=placed, out_specs=P("row", "col"), check_vma=False
    )
```

```python
import functools

import jax
import jax.numpy as jnp
from jax import lax
from jax.experimental import pallas as pl
from jax.experimental.pallas import tpu as pltpu
from jax.sharding import PartitionSpec as P

BLK = 96
TILE = 384
NROW = 16
ORBD = 24
LANES = 128
RING = 8
HIGH = lax.Precision.HIGHEST
F32 = jnp.float32
VMEM = pl.BlockSpec(memory_space=pltpu.VMEM)
SMEM = pl.BlockSpec(memory_space=pltpu.SMEM)
ANY = pl.BlockSpec(memory_space=pl.ANY)


def iota(shape, dim):
    return lax.broadcasted_iota(jnp.int32, shape, dim)


def position(index):
    row, col = divmod(index, NROW)
    return row // RING, row % RING, col // RING, col % RING // 2, col % 2


def groups(key):
    found = {}
    for index in range(NROW * NROW):
        found.setdefault(key(*position(index)), []).append(index)
    return list(found.values())


PLANE = groups(lambda xh, z, xl, y, core: (z, core))
PILLAR = groups(lambda xh, z, xl, y, core: (xh, xl, y))


def pack_kernel(charges, hubbard, picks, mask, out):
    values = [charges[i, j] for i in range(3) for j in range(4)]
    values += [hubbard[i, j] for i in range(3) for j in range(4)]
    values += [picks[0, 0, o].astype(F32) for o in range(ORBD)]
    values += [mask[i, j].astype(F32) for i in range(4) for j in range(4)]
    lane = iota((1, LANES), 1)
    row = jnp.zeros((1, LANES), F32)
    for n, value in enumerate(values):
        row = jnp.where(lane == n, value, row)
    for n in range(NROW):
        out[n] = row


def pack(charges, hubbard, orbital_atom, block_mask):
    return pl.pallas_call(
        pack_kernel,
        out_shape=jax.ShapeDtypeStruct((NROW, 1, LANES), F32),
        in_specs=[SMEM, SMEM, SMEM, SMEM],
        out_specs=VMEM,
    )(charges, hubbard, orbital_atom, block_mask)


def copy_kernel(parts, bare_other, inter_other, out):
    rows = jnp.concatenate([parts[n] for n in range(NROW)], axis=0)
    for n in range(NROW):
        out[n] = rows


def copies_of(parts, bare_other, inter_other):
    return pl.pallas_call(
        copy_kernel,
        out_shape=jax.ShapeDtypeStruct((NROW, NROW, LANES), F32),
        in_specs=[VMEM, ANY, ANY],
        out_specs=VMEM,
    )(parts, bare_other, inter_other)


def exchange(copies, members):
    return lax.all_to_all(copies, ("row", "col"), 0, 0, axis_index_groups=members)


def spread_of():
    value = iota((LANES, LANES), 0)
    lane = iota((LANES, LANES), 1)
    parts = [value == 4 * i + lane % 4 for i in range(6)]
    parts += [value == 24 + (lane + LANES * i) % ORBD for i in range(3)]
    parts += [value == 48 + 4 * i + lane % 4 for i in range(4)]
    return jnp.concatenate([part.astype(F32) for part in parts], axis=1)


def domain_row(parts, spread, q):
    half, z = q // RING, q % RING
    domain = iota((NROW, LANES), 0)
    lane = iota((NROW, LANES), 1)
    block = parts[pl.ds(half * RING, RING), pl.ds(z * 2, 2), :]
    block = jnp.concatenate([block[n // 2, n % 2 : n % 2 + 1] for n in range(NROW)], axis=0)
    wide = jnp.dot(block, spread, precision=HIGH, preferred_element_type=F32)
    rows = []
    for i in range(13):
        here = lane % 64 // 4 == domain
        if 6 <= i < 9:
            here = (lane + LANES * (i - 6)) // ORBD == domain
        piece = wide[:, i * LANES : (i + 1) * LANES]
        rows.append(jnp.sum(jnp.where(here, piece, 0.0), axis=0, keepdims=True))
    return rows


def row_shift(above, here, below, coupling):
    atoms = [above[2], here[0], here[1], here[2], below[0]]
    rolled = [[pltpu.roll(v, 1, 1), v, pltpu.roll(v, LANES - 1, 1)] for v in atoms]
    grids = []
    for i in range(3):
        shift = here[3 + i] * here[i]
        for a in range(3):
            for b in range(3):
                shift = shift + coupling[a, b] * rolled[i + a][b]
        grids.append(shift)
    line = iota((8, LANES), 0)
    grid = jnp.where(line == 0, grids[0], jnp.where(line == 1, grids[1], jnp.where(line == 2, grids[2], 0.0)))
    picks = jnp.concatenate(here[6:9], axis=1).astype(jnp.int32)
    orbital = iota((1, TILE), 1)
    atom_row = picks // 4
    atom_col = 4 * (orbital // ORBD) + picks % 4
    onehot = (iota((LANES, TILE), 0) == atom_col).astype(F32)
    by_row = jnp.dot(grid, onehot, precision=HIGH, preferred_element_type=F32)
    return jnp.sum(jnp.where(iota((8, TILE), 0) == atom_row, by_row, 0.0), axis=0, keepdims=True)


def as_column(shift):
    return jnp.broadcast_to(shift, (LANES, TILE)).T


def kept(here, col):
    blocks = jnp.concatenate(here[9:13] * 2, axis=0)
    onehot = (iota((LANES, TILE), 0) == 4 * col + iota((LANES, TILE), 1) // BLK).astype(F32)
    return jnp.dot(blocks, onehot, preferred_element_type=F32)


def form(out, bare, inter, keep, down, along, diagonal):
    for i in range(TILE // BLK):
        rows = slice(i * BLK, (i + 1) * BLK)
        ham = bare[rows, :].astype(F32) + 0.5 * inter[rows, :].astype(F32) * (down[rows, :1] + along)
        eye = jnp.where(iota((BLK, TILE), 0) + i * BLK == iota((BLK, TILE), 1), diagonal, 0.0)
        out[rows, :] = (eye - keep[i : i + 1] * ham).astype(jnp.bfloat16)


def initial_kernel(parts, coupling, bare, inter, bare_other, inter_other, out, out_other):
    row, col = lax.axis_index("row"), lax.axis_index("col")
    spread = spread_of()

    def around(q):
        return [domain_row(parts, spread, (q + by) % NROW) for by in (NROW - 1, 0, 1)]

    along = row_shift(*around(col), coupling)
    for q, ham, overlap, to in ((row, bare, inter, out), ((row + RING) % NROW, bare_other, inter_other, out_other)):
        near = around(q)
        down = as_column(row_shift(*near, coupling))
        form(to, ham, overlap, kept(near[1], col), down, along, jnp.where(q == col, 0.5, 0.0))


BIG = pltpu.CompilerParams(vmem_limit_bytes=62 << 20)


def initial_tiles(parts, coupling, *sources):
    return pl.pallas_call(
        initial_kernel,
        out_shape=[jax.ShapeDtypeStruct((TILE, TILE), jnp.bfloat16)] * 2,
        in_specs=[VMEM, SMEM] + [VMEM] * 4,
        out_specs=[VMEM, VMEM],
        compiler_params=BIG,
    )(parts, coupling, *sources)


def ring_step(value, by):
    return lax.ppermute(value, "row", [(h * RING + i, h * RING + (i + by) % RING) for h in range(2) for i in range(RING)])


def swap_half(value):
    return lax.ppermute(value, "row", [(i, i ^ RING) for i in range(NROW)])


def column_tiles(tile, other):
    found = {(0, 0): tile, (1, 0): other}
    up, down = [tile, other], [tile, other]
    for step in (1, 2, 3):
        for half in (0, 1):
            up[half] = ring_step(up[half], 1)
            down[half] = ring_step(down[half], -1)
            found[half, step] = up[half]
            found[half, RING - step] = down[half]
    found[0, 4] = ring_step(up[0], 1)
    found[1, 4] = ring_step(down[1], -1)
    return found


def plane_step(value, flip, by):
    pairs = []
    for index in range(NROW):
        half, y, core = index // RING, index % RING // 2, index % 2
        pairs.append((index, (half ^ flip) * RING + (y + by) % 4 * 2 + core))
    return lax.ppermute(value, "col", pairs)


def swap_core(value):
    return lax.ppermute(value, "col", [(i, i ^ 1) for i in range(NROW)])


def square_tiles(tile):
    other = plane_step(tile, 1, 0)
    found = [(0, 0, tile), (1, 0, other)]
    for by in (1, 3, 2):
        found.append((0, by, plane_step(tile, 0, by)))
    far = found[-1][2]
    far, _ = lax.optimization_barrier((far, other))
    for by in (1, 3):
        found.append((1, by, plane_step(other, 0, by)))
    found.append((1, 2, plane_step(far, 1, 0)))
    return [(flip, by, side, swap_core(value) if side else value) for flip, by, value in found for side in (0, 1)]


def run(copies):
    for copy in copies:
        copy.start()
    return copies


def settle(copies):
    for copy in copies:
        copy.wait()


def square_kernel(places, first, *refs):
    count = len(places)
    strip_ref, *refs = refs
    held = [] if first else [refs.pop(0)]
    tile_refs, refs = refs[:count], refs[count:]
    outs, (strip, column, sems) = refs[:-3], refs[-3:]
    row = lax.axis_index("row")
    own, z = row // RING, row % RING
    copies = []
    for n, (half, distance) in enumerate(places):
        k = (own + half) % 2 * RING + (z - distance + RING) % RING
        source = strip_ref.at[:, pl.ds(pl.multiple_of(k * TILE, TILE), TILE)]
        copies.append(pltpu.make_async_copy(tile_refs[n], column.at[n * TILE : (n + 1) * TILE, :], sems.at[2 * n]))
        copies.append(pltpu.make_async_copy(source, strip.at[:, n * TILE : (n + 1) * TILE], sems.at[2 * n + 1]))
    run(copies)
    for n in range(0, count, 4):
        upto = min(n + 4, count)
        settle(copies[2 * n : 2 * upto])
        span = slice(n * TILE, upto * TILE)
        part = jnp.dot(strip[:, span], column[span, :], preferred_element_type=F32)
        if n == 0 and not held:
            outs[0][...] = part
        else:
            outs[0][...] = (held[0][...] if n == 0 else outs[0][...]) + part
    if not first:
        outs[1][...] = outs[0][...].astype(jnp.bfloat16)


def square_of(strip, held, found, places):
    count = len(places)
    shapes = [jax.ShapeDtypeStruct((TILE, TILE), F32)]
    if held:
        shapes.append(jax.ShapeDtypeStruct((TILE, TILE), jnp.bfloat16))
    return pl.pallas_call(
        functools.partial(square_kernel, places, not held),
        out_shape=shapes,
        in_specs=[ANY] + [VMEM] * len(held) + [ANY] * count,
        out_specs=[VMEM] * len(shapes),
        scratch_shapes=[
            pltpu.VMEM((TILE, count * TILE), jnp.bfloat16),
            pltpu.VMEM((count * TILE, TILE), jnp.bfloat16),
            pltpu.SemaphoreType.DMA((2 * count,)),
        ],
        compiler_params=BIG,
        cost_estimate=cost(count),
    )(strip, *held, *[found[place] for place in places])


def cost(count):
    return pl.CostEstimate(flops=2 * count * TILE**3, bytes_accessed=4 * count * TILE**2, transcendentals=0)


ORDER = tuple((half, 2 * step + odd) for odd in (0, 1) for half in (0, 1) for step in range(4))
LAST = ((0, 4), (1, 4))
FIRST = tuple(place for place in ORDER if place not in LAST)


def rows_for(flip, by, side):
    row, col = lax.axis_index("row"), lax.axis_index("col")
    k = (col // RING + flip) % 2 * RING + (col % RING // 2 - by + 4) % 4 * 2 + (col + side) % 2
    half, distance = (k // RING + row // RING) % 2, (row % RING - k % RING + RING) % RING
    return pl.ds(pl.multiple_of((distance % 2 * 8 + half * 4 + distance // 2) * TILE, TILE), TILE)


def cube_kernel(places, square_ref, *refs):
    tile_refs, column_refs, refs = refs[:NROW], refs[NROW : 2 * NROW], refs[2 * NROW :]
    out, square, strip, column, sems = refs
    copies = [pltpu.make_async_copy(ref, strip.at[:, rows_for(*place)], sems.at[n]) for n, (ref, place) in enumerate(zip(tile_refs, places))]
    for n, ref in enumerate(column_refs):
        copies.append(pltpu.make_async_copy(ref, column.at[n * TILE : (n + 1) * TILE, :], sems.at[NROW + n]))
    copies.append(pltpu.make_async_copy(square_ref, square, sems.at[2 * NROW]))
    run(copies)
    settle(copies[:NROW])
    for n in range(0, NROW, 4):
        settle(copies[NROW + n : NROW + n + 4])
        span = slice(n * TILE, (n + 4) * TILE)
        part = jnp.dot(strip[:, span], column[span, :], preferred_element_type=F32)
        if n == 0:
            out[...] = part
        elif n < NROW - 4:
            out[...] += part
        else:
            settle(copies[2 * NROW :])
            out[...] = 3.0 * square[...] - 2.0 * (out[...] + part)


def cube_of(square, tiles, columns, places):
    return pl.pallas_call(
        functools.partial(cube_kernel, places),
        out_shape=jax.ShapeDtypeStruct((TILE, TILE), F32),
        in_specs=[ANY] * (1 + 2 * NROW),
        out_specs=VMEM,
        scratch_shapes=[
            pltpu.VMEM((TILE, TILE), F32),
            pltpu.VMEM((TILE, NROW * TILE), jnp.bfloat16),
            pltpu.VMEM((NROW * TILE, TILE), jnp.bfloat16),
            pltpu.SemaphoreType.DMA((2 * NROW + 1,)),
        ],
        compiler_params=BIG,
        cost_estimate=cost(NROW),
    )(square, *tiles, *columns)


def per_device(charges, hubbard, coupling, orbital_atom, block_mask, bare_ham, intersection):
    bare_other, intersection_other = swap_half(bare_ham), swap_half(intersection)
    parts = exchange(pack(charges, hubbard, orbital_atom, block_mask), PILLAR)
    parts = exchange(copies_of(parts, bare_other, intersection_other), PLANE)
    initial, initial_other = initial_tiles(parts, coupling, bare_ham, intersection, bare_other, intersection_other)
    initial_strip = lax.all_gather(initial, "col", axis=1, tiled=True)
    found = column_tiles(initial, initial_other)
    held = square_of(initial_strip, [], found, FIRST)
    square, square_low = square_of(initial_strip, held, found, LAST)
    tiles = square_tiles(square_low)
    places, values = [tile[:3] for tile in tiles], [tile[3] for tile in tiles]
    return cube_of(square, values, [found[place] for place in ORDER], places)


def solution(mesh):
    placed = (
        P("row", "col"),
        P("row", "col"),
        P(),
        P("row", "col", None),
        P("row", "col"),
        P("row", "col"),
        P("row", "col"),
    )
    return jax.shard_map(
        per_device, mesh=mesh, in_specs=placed, out_specs=P("row", "col"), check_vma=False
    )
```

```python
import functools

import jax
import jax.numpy as jnp
from jax import lax
from jax.experimental import pallas as pl
from jax.experimental.pallas import tpu as pltpu
from jax.sharding import PartitionSpec as P

BLK = 96
TILE = 384
NROW = 16
ORBD = 24
LANES = 128
RING = 8
HIGH = lax.Precision.HIGHEST
F32 = jnp.float32
VMEM = pl.BlockSpec(memory_space=pltpu.VMEM)
SMEM = pl.BlockSpec(memory_space=pltpu.SMEM)
ANY = pl.BlockSpec(memory_space=pl.ANY)


def iota(shape, dim):
    return lax.broadcasted_iota(jnp.int32, shape, dim)


def position(index):
    row, col = divmod(index, NROW)
    return row // RING, row % RING, col // RING, col % RING // 2, col % 2


def groups(key):
    found = {}
    for index in range(NROW * NROW):
        found.setdefault(key(*position(index)), []).append(index)
    return list(found.values())


PLANE = groups(lambda xh, z, xl, y, core: (z, core))
PILLAR = groups(lambda xh, z, xl, y, core: (xh, xl, y))


def pack_kernel(charges, hubbard, picks, mask, out):
    values = [charges[i, j] for i in range(3) for j in range(4)]
    values += [hubbard[i, j] for i in range(3) for j in range(4)]
    values += [picks[0, 0, o].astype(F32) for o in range(ORBD)]
    values += [mask[i, j].astype(F32) for i in range(4) for j in range(4)]
    lane = iota((1, LANES), 1)
    row = jnp.zeros((1, LANES), F32)
    for n, value in enumerate(values):
        row = jnp.where(lane == n, value, row)
    for n in range(NROW):
        out[n] = row


def pack(charges, hubbard, orbital_atom, block_mask):
    return pl.pallas_call(
        pack_kernel,
        out_shape=jax.ShapeDtypeStruct((NROW, 1, LANES), F32),
        in_specs=[SMEM, SMEM, SMEM, SMEM],
        out_specs=VMEM,
    )(charges, hubbard, orbital_atom, block_mask)


def copy_kernel(parts, bare_other, inter_other, out):
    rows = jnp.concatenate([parts[n] for n in range(NROW)], axis=0)
    for n in range(NROW):
        out[n] = rows


def copies_of(parts, bare_other, inter_other):
    return pl.pallas_call(
        copy_kernel,
        out_shape=jax.ShapeDtypeStruct((NROW, NROW, LANES), F32),
        in_specs=[VMEM, ANY, ANY],
        out_specs=VMEM,
    )(parts, bare_other, inter_other)


def exchange(copies, members):
    return lax.all_to_all(copies, ("row", "col"), 0, 0, axis_index_groups=members)


def spread_of():
    value = iota((LANES, LANES), 0)
    lane = iota((LANES, LANES), 1)
    parts = [value == 4 * i + lane % 4 for i in range(6)]
    parts += [value == 24 + (lane + LANES * i) % ORBD for i in range(3)]
    parts += [value == 48 + 4 * i + lane % 4 for i in range(4)]
    return jnp.concatenate([part.astype(F32) for part in parts], axis=1)


def domain_row(parts, spread, q, wanted=range(13)):
    half, z = q // RING, q % RING
    domain = iota((NROW, LANES), 0)
    lane = iota((NROW, LANES), 1)
    block = parts[pl.ds(half * RING, RING), pl.ds(z * 2, 2), :]
    block = jnp.concatenate([block[n // 2, n % 2 : n % 2 + 1] for n in range(NROW)], axis=0)
    start = wanted[0]
    lanes = slice(start * LANES, (start + len(wanted)) * LANES)
    wide = jnp.dot(block, spread[:, lanes], precision=HIGH, preferred_element_type=F32)
    rows = []
    for i in wanted:
        here = lane % 64 // 4 == domain
        if 6 <= i < 9:
            here = (lane + LANES * (i - 6)) // ORBD == domain
        piece = wide[:, (i - start) * LANES : (i - start + 1) * LANES]
        rows.append(jnp.sum(jnp.where(here, piece, 0.0), axis=0, keepdims=True))
    return rows


def row_shift(above, here, below, coupling):
    atoms = [above[0], here[0], here[1], here[2], below[0]]
    rolled = [[pltpu.roll(v, 1, 1), v, pltpu.roll(v, LANES - 1, 1)] for v in atoms]
    grids = []
    for i in range(3):
        shift = here[3 + i] * here[i]
        for a in range(3):
            for b in range(3):
                shift = shift + coupling[a, b] * rolled[i + a][b]
        grids.append(shift)
    line = iota((8, LANES), 0)
    grid = jnp.where(line == 0, grids[0], jnp.where(line == 1, grids[1], jnp.where(line == 2, grids[2], 0.0)))
    picks = jnp.concatenate(here[6:9], axis=1).astype(jnp.int32)
    orbital = iota((1, TILE), 1)
    atom_row = picks // 4
    atom_col = 4 * (orbital // ORBD) + picks % 4
    onehot = (iota((LANES, TILE), 0) == atom_col).astype(F32)
    by_row = jnp.dot(grid, onehot, precision=HIGH, preferred_element_type=F32)
    return jnp.sum(jnp.where(iota((8, TILE), 0) == atom_row, by_row, 0.0), axis=0, keepdims=True)


def as_column(shift):
    return jnp.broadcast_to(shift, (LANES, TILE)).T


def kept(here, col):
    blocks = jnp.concatenate(here[9:13] * 2, axis=0)
    onehot = (iota((LANES, TILE), 0) == 4 * col + iota((LANES, TILE), 1) // BLK).astype(F32)
    return jnp.dot(blocks, onehot, preferred_element_type=F32)


def form(out, bare, inter, keep, down, along, diagonal):
    for i in range(TILE // BLK):
        rows = slice(i * BLK, (i + 1) * BLK)
        ham = bare[rows, :].astype(F32) + 0.5 * inter[rows, :].astype(F32) * (down[rows, :1] + along)
        eye = jnp.where(iota((BLK, TILE), 0) + i * BLK == iota((BLK, TILE), 1), diagonal, 0.0)
        out[rows, :] = (eye - keep[i : i + 1] * ham).astype(jnp.bfloat16)


def initial_kernel(parts, coupling, bare, inter, bare_other, inter_other, out, out_other):
    row, col = lax.axis_index("row"), lax.axis_index("col")
    spread = spread_of()

    def around(q):
        above = domain_row(parts, spread, (q + NROW - 1) % NROW, range(2, 3))
        return above, domain_row(parts, spread, q), domain_row(parts, spread, (q + 1) % NROW, range(1))

    along = row_shift(*around(col), coupling)
    for q, ham, overlap, to in ((row, bare, inter, out), ((row + RING) % NROW, bare_other, inter_other, out_other)):
        near = around(q)
        down = as_column(row_shift(*near, coupling))
        form(to, ham, overlap, kept(near[1], col), down, along, jnp.where(q == col, 0.5, 0.0))


BIG = pltpu.CompilerParams(vmem_limit_bytes=62 << 20)


def initial_tiles(parts, coupling, *sources):
    return pl.pallas_call(
        initial_kernel,
        out_shape=[jax.ShapeDtypeStruct((TILE, TILE), jnp.bfloat16)] * 2,
        in_specs=[VMEM, SMEM] + [VMEM] * 4,
        out_specs=[VMEM, VMEM],
        compiler_params=BIG,
    )(parts, coupling, *sources)


def ring_step(value, by):
    return lax.ppermute(value, "row", [(h * RING + i, h * RING + (i + by) % RING) for h in range(2) for i in range(RING)])


def swap_half(value):
    return lax.ppermute(value, "row", [(i, i ^ RING) for i in range(NROW)])


def column_tiles(tile, other):
    found = {(0, 0): tile, (1, 0): other}
    up, down = [tile, other], [tile, other]
    for step in (1, 2, 3):
        for half in (0, 1):
            up[half] = ring_step(up[half], 1)
            down[half] = ring_step(down[half], -1)
            found[half, step] = up[half]
            found[half, RING - step] = down[half]
    found[0, 4] = ring_step(up[0], 1)
    found[1, 4] = ring_step(down[1], -1)
    return found


def plane_step(value, flip, by):
    pairs = []
    for index in range(NROW):
        half, y, core = index // RING, index % RING // 2, index % 2
        pairs.append((index, (half ^ flip) * RING + (y + by) % 4 * 2 + core))
    return lax.ppermute(value, "col", pairs)


def swap_core(value):
    return lax.ppermute(value, "col", [(i, i ^ 1) for i in range(NROW)])


def square_tiles(tile):
    other = plane_step(tile, 1, 0)
    found = [(0, 0, tile), (1, 0, other)]
    for by in (1, 3, 2):
        found.append((0, by, plane_step(tile, 0, by)))
    far = found[-1][2]
    far, _ = lax.optimization_barrier((far, other))
    for by in (1, 3):
        found.append((1, by, plane_step(other, 0, by)))
    found.append((1, 2, plane_step(far, 1, 0)))
    return [(flip, by, side, swap_core(value) if side else value) for flip, by, value in found for side in (0, 1)]


def run(copies):
    for copy in copies:
        copy.start()
    return copies


def settle(copies):
    for copy in copies:
        copy.wait()


def square_kernel(places, first, *refs):
    count = len(places)
    strip_ref, *refs = refs
    held = [] if first else [refs.pop(0)]
    tile_refs, refs = refs[:count], refs[count:]
    outs, (strip, column, sems) = refs[:-3], refs[-3:]
    row = lax.axis_index("row")
    own, z = row // RING, row % RING
    copies = []
    for n, (half, distance) in enumerate(places):
        k = (own + half) % 2 * RING + (z - distance + RING) % RING
        source = strip_ref.at[:, pl.ds(pl.multiple_of(k * TILE, TILE), TILE)]
        copies.append(pltpu.make_async_copy(tile_refs[n], column.at[n * TILE : (n + 1) * TILE, :], sems.at[2 * n]))
        copies.append(pltpu.make_async_copy(source, strip.at[:, n * TILE : (n + 1) * TILE], sems.at[2 * n + 1]))
    run(copies)
    for n in range(0, count, 2):
        upto = min(n + 2, count)
        settle(copies[2 * n : 2 * upto])
        span = slice(n * TILE, upto * TILE)
        part = jnp.dot(strip[:, span], column[span, :], preferred_element_type=F32)
        if n == 0 and not held:
            outs[0][...] = part
        else:
            outs[0][...] = (held[0][...] if n == 0 else outs[0][...]) + part
    if not first:
        outs[1][...] = outs[0][...].astype(jnp.bfloat16)


def square_of(strip, held, found, places):
    count = len(places)
    shapes = [jax.ShapeDtypeStruct((TILE, TILE), F32)]
    if held:
        shapes.append(jax.ShapeDtypeStruct((TILE, TILE), jnp.bfloat16))
    return pl.pallas_call(
        functools.partial(square_kernel, places, not held),
        out_shape=shapes,
        in_specs=[ANY] + [VMEM] * len(held) + [ANY] * count,
        out_specs=[VMEM] * len(shapes),
        scratch_shapes=[
            pltpu.VMEM((TILE, count * TILE), jnp.bfloat16),
            pltpu.VMEM((count * TILE, TILE), jnp.bfloat16),
            pltpu.SemaphoreType.DMA((2 * count,)),
        ],
        compiler_params=pltpu.CompilerParams(vmem_limit_bytes=16 << 20),
        cost_estimate=cost(count),
    )(strip, *held, *[found[place] for place in places])


def cost(count):
    return pl.CostEstimate(flops=2 * count * TILE**3, bytes_accessed=4 * count * TILE**2, transcendentals=0)


ORDER = tuple((half, 2 * step + odd) for odd in (0, 1) for half in (0, 1) for step in range(4))
LAST = ((0, 4), (1, 4))
FIRST = tuple(place for place in ORDER if place not in LAST)


def rows_for(flip, by, side):
    row, col = lax.axis_index("row"), lax.axis_index("col")
    k = (col // RING + flip) % 2 * RING + (col % RING // 2 - by + 4) % 4 * 2 + (col + side) % 2
    half, distance = (k // RING + row // RING) % 2, (row % RING - k % RING + RING) % RING
    return pl.ds(pl.multiple_of((distance % 2 * 8 + half * 4 + distance // 2) * TILE, TILE), TILE)


def cube_kernel(places, square_ref, *refs):
    tile_refs, column_refs, refs = refs[:NROW], refs[NROW : 2 * NROW], refs[2 * NROW :]
    out, square, strip, column, sems = refs
    copies = [pltpu.make_async_copy(ref, strip.at[:, rows_for(*place)], sems.at[n]) for n, (ref, place) in enumerate(zip(tile_refs, places))]
    for n, ref in enumerate(column_refs):
        copies.append(pltpu.make_async_copy(ref, column.at[n * TILE : (n + 1) * TILE, :], sems.at[NROW + n]))
    copies.append(pltpu.make_async_copy(square_ref, square, sems.at[2 * NROW]))
    run(copies)
    settle(copies[:NROW])
    for n in range(0, NROW, 2):
        settle(copies[NROW + n : NROW + n + 2])
        span = slice(n * TILE, (n + 2) * TILE)
        part = jnp.dot(strip[:, span], column[span, :], preferred_element_type=F32)
        if n == 0:
            out[...] = part
        elif n < NROW - 2:
            out[...] += part
        else:
            settle(copies[2 * NROW :])
            out[...] = 3.0 * square[...] - 2.0 * (out[...] + part)


def cube_of(square, tiles, columns, places):
    return pl.pallas_call(
        functools.partial(cube_kernel, places),
        out_shape=jax.ShapeDtypeStruct((TILE, TILE), F32),
        in_specs=[ANY] * (1 + 2 * NROW),
        out_specs=VMEM,
        scratch_shapes=[
            pltpu.VMEM((TILE, TILE), F32),
            pltpu.VMEM((TILE, NROW * TILE), jnp.bfloat16),
            pltpu.VMEM((NROW * TILE, TILE), jnp.bfloat16),
            pltpu.SemaphoreType.DMA((2 * NROW + 1,)),
        ],
        compiler_params=pltpu.CompilerParams(vmem_limit_bytes=16 << 20),
        cost_estimate=cost(NROW),
    )(square, *tiles, *columns)


def per_device(charges, hubbard, coupling, orbital_atom, block_mask, bare_ham, intersection):
    bare_other, intersection_other = swap_half(bare_ham), swap_half(intersection)
    parts = exchange(pack(charges, hubbard, orbital_atom, block_mask), PILLAR)
    parts = exchange(copies_of(parts, bare_other, intersection_other), PLANE)
    initial, initial_other = initial_tiles(parts, coupling, bare_ham, intersection, bare_other, intersection_other)
    initial_strip = lax.all_gather(initial, "col", axis=1, tiled=True)
    found = column_tiles(initial, initial_other)
    held = square_of(initial_strip, [], found, FIRST)
    square, square_low = square_of(initial_strip, held, found, LAST)
    tiles = square_tiles(square_low)
    places, values = [tile[:3] for tile in tiles], [tile[3] for tile in tiles]
    return cube_of(square, values, [found[place] for place in ORDER], places)


def solution(mesh):
    placed = (
        P("row", "col"),
        P("row", "col"),
        P(),
        P("row", "col", None),
        P("row", "col"),
        P("row", "col"),
        P("row", "col"),
    )
    return jax.shard_map(
        per_device, mesh=mesh, in_specs=placed, out_specs=P("row", "col"), check_vma=False
    )
```
